128 devices in a mesh: layer: 8 (over z, core), grid: 16 (over x, y).
Axes of the slice: x: 4, y: 4, z: 4, core: 2. Of those that a mesh axis runs over, the one named last changes fastest.
Arguments:
- leaf_rhs: float32 [1024, 256, 256], P(('layer', 'grid')), may hold values from -6 to 6
- leaf_linv: float32 [1024, 256, 256], P(('layer', 'grid')), as said below
- leaf_uinv: float32 [1024, 256, 256], P(('layer', 'grid')), as said below
- low_couple: float32 [1024, 2, 256, 256], P(('layer', 'grid')), may hold values from -0.09375 to 0.09375
- up_couple: float32 [1024, 2, 256, 256], P(('layer', 'grid')), may hold values from -0.25 to 0.25
- targets: int32 [1024, 2], P(('layer', 'grid')), may hold values from 0 to 31, all different within a row
- top_rhs: float32 [32, 256, 256], P('grid'), may hold values from -6 to 6
- top_linv: float32 [32, 256, 256], P('grid'), as said below
- top_uinv: float32 [32, 256, 256], P('grid'), as said below
- top_lower: float32 [32, 256, 256], P('grid'), may hold values from -0.375 to 0.375
- top_upper: float32 [32, 256, 256], P('grid'), may hold values from -0.375 to 0.375
Outputs:
- leaf_sol: float32 [1024, 256, 256], P(('layer', 'grid'))
- top_sol: float32 [32, 256, 256], P('grid')
The draws below stay inside these ranges and needn't reach their ends.
Inputs may be any that keep to these rules, and one draw needn't show every extreme that they name: The 2 targets of one subtree supernode are distinct, and every ancestor is named by some coupling block. `leaf_linv`: unit lower triangular tiles. `leaf_uinv`: upper triangular tiles with positive diagonal. `top_linv`: unit lower triangular tiles. `top_uinv`: upper triangular tiles with positive diagonal.
All inputs are finite; a program needn't handle non-finite values.
Results may differ from the reference program's by a relative error of at most 0.00028.
Values sent between devices are 32-bit elements; how exact they have to be, the bound alone decides.
No kernel may reach another device: no remote copies, remote signals or barrier semaphores. Data moves between devices by JAX's collectives and lax.ppermute only.
A program may use at most 128 MiB of HBM per device.

```python
import jax
import jax.numpy as jnp
from jax import lax

B = 256
NRHS = 256
NCOUP = 2
LEAVES = 1024
TOP = 32


def jitter_tiles(key, count):
    values = jax.random.normal(key, (count, B, B), jnp.float32)
    return values * (0.5 / B ** 0.5)


def unit_lower(key, count):
    values = jitter_tiles(key, count)
    return jnp.tril(values, -1) + jnp.eye(B, dtype=jnp.float32)[None, :, :]


def upper_tiles(key, count):
    values = jitter_tiles(jax.random.fold_in(key, 3), count)
    diagonal = jax.random.uniform(jax.random.fold_in(key, 5), (count, B), jnp.float32, 0.7, 1.3)
    return jnp.triu(values, 1) + diagonal[:, :, None] * jnp.eye(B, dtype=jnp.float32)[None, :, :]


def draw_leaf_linv(key, part):
    return unit_lower(jax.random.fold_in(key, 11), LEAVES)


def draw_leaf_uinv(key, part):
    return upper_tiles(jax.random.fold_in(key, 13), LEAVES)


def draw_top_linv(key, part):
    return unit_lower(jax.random.fold_in(key, 17), TOP)


def draw_top_uinv(key, part):
    return upper_tiles(jax.random.fold_in(key, 19), TOP)


def levels(own_key, dims, cuts, low, largest):
    def one(dim, blocks):
        heights = jax.random.uniform(jax.random.fold_in(jax.random.fold_in(own_key, 6), dim), (blocks,), jnp.float32, low / len(cuts), largest / len(cuts))
        return jnp.repeat(jnp.exp(heights), dims[dim] // blocks).reshape((-1,) + (1,) * (len(dims) - dim - 1))

    gain = one(*cuts[0])
    for cut in cuts[1:]:
        gain = gain * one(*cut)
    return gain


def distinct(key, rows, amount, top, lift):
    ranking = jax.random.permutation(jax.random.fold_in(key, 1), amount)
    favour = ranking
    for power in range(3):
        favour = favour * favour // amount
    favour = favour * lift // amount
    tickets = jax.random.randint(jax.random.fold_in(key, 2), (rows, amount), 0, 4096) + favour
    sure = jax.random.permutation(jax.random.fold_in(key, 3), rows)[jnp.arange(amount) % rows]
    tickets = jnp.where(jnp.arange(rows)[:, None] == sure[None, :], 1 << 14, tickets)
    priority = tickets * amount + jnp.arange(amount)
    return lax.top_k(priority.astype(jnp.int32), top)[1].astype(jnp.int32)


def scatter_about(key, shape, spread, limit, pieces=(), kind=jnp.bfloat16):
    drawn = spread * jax.random.normal(key, shape, jnp.float32)
    if pieces:
        drawn = drawn * levels(key, shape, pieces, -0.22, 0.18)
    return jnp.clip(drawn, -limit, limit).astype(kind)


def setup_inputs(seed: int = 0) -> dict:
    seeds = jax.random.split(jax.random.key(seed), 12)
    leaf_rhs = scatter_about(seeds[0], (LEAVES, B, NRHS), 1.0, 6.0, ((0, 128),), jnp.float32)
    leaf_linv = draw_leaf_linv(jax.random.fold_in(seeds[11], 71), 0)
    leaf_uinv = draw_leaf_uinv(jax.random.fold_in(seeds[11], 71), 0)
    low_couple = scatter_about(seeds[3], (LEAVES, NCOUP, B, B), (B * 16) ** -0.5, 0.09375, ((0, 128),), jnp.float32)
    up_couple = scatter_about(seeds[4], (LEAVES, NCOUP, B, B), (B * NCOUP) ** -0.5, 0.25, ((0, 128),), jnp.float32)
    targets = distinct(seeds[5], LEAVES, TOP, NCOUP, 1024)
    top_rhs = scatter_about(seeds[6], (TOP, B, NRHS), 1.0, 6.0, ((0, 16),), jnp.float32)
    top_linv = draw_top_linv(jax.random.fold_in(seeds[11], 71), 0)
    top_uinv = draw_top_uinv(jax.random.fold_in(seeds[11], 71), 0)
    top_lower = scatter_about(seeds[9], (TOP, B, B), (B + B // 8) ** -0.5, 0.375, ((0, 16),), jnp.float32)
    top_upper = scatter_about(seeds[10], (TOP, B, B), (B + B // 8) ** -0.5, 0.375, ((0, 16),), jnp.float32)
    return dict(leaf_rhs=leaf_rhs, leaf_linv=leaf_linv, leaf_uinv=leaf_uinv, low_couple=low_couple, up_couple=up_couple, targets=targets, top_rhs=top_rhs, top_linv=top_linv, top_uinv=top_uinv, top_lower=top_lower, top_upper=top_upper)


highest = lax.Precision.HIGHEST


def reference(leaf_rhs, leaf_linv, leaf_uinv, low_couple, up_couple, targets, top_rhs, top_linv, top_uinv, top_lower, top_upper):
    leaf_fwd = jnp.einsum("kij,kjr->kir", leaf_linv, leaf_rhs, precision=highest)

    def gather_terms(running, record):
        couple, forward, where = record
        terms = jnp.einsum("cij,jr->cir", couple, forward, precision=highest)
        return running.at[where].add(terms), None

    partial_value, _ = lax.scan(gather_terms, jnp.zeros(top_rhs.shape, jnp.float32), (low_couple, leaf_fwd, targets))
    reduced = top_rhs - partial_value

    def down_step(previous, record):
        inverse, lower, source = record
        current = jnp.dot(inverse, source - jnp.dot(lower, previous, precision=highest), precision=highest)
        return current, current

    _, top_fwd = lax.scan(down_step, jnp.zeros(top_rhs.shape[1:], jnp.float32), (top_linv, top_lower, reduced))

    def up_step(following, record):
        inverse, upper, source = record
        current = jnp.dot(inverse, source - jnp.dot(upper, following, precision=highest), precision=highest)
        return current, current

    _, top_sol = lax.scan(up_step, jnp.zeros(top_rhs.shape[1:], jnp.float32), (top_uinv, top_upper, top_fwd), reverse=True)

    def leaf_back(record):
        inverse, couple, where, forward = record
        picked = top_sol[where]
        correction = jnp.einsum("cij,cjr->ir", couple, picked, precision=highest)
        return jnp.dot(inverse, forward - correction, precision=highest)

    leaf_sol = lax.map(leaf_back, (leaf_uinv, up_couple, targets, leaf_fwd))
    return leaf_sol, top_sol
```

```python
import functools

import jax
import jax.numpy as jnp
from jax import lax
from jax.experimental import pallas as pl
from jax.experimental.pallas import tpu as pltpu
from jax.sharding import PartitionSpec as P

LAYERS = 8
GRID = 16
TILE = 256
COLS = TILE // LAYERS
TOPS = 32
VMEM_LIMIT = 56 * 1024 * 1024

NN = (((1,), (0,)), ((), ()))
NT = (((1,), (1,)), ((), ()))

whole = pl.BlockSpec(memory_space=pltpu.VMEM)
in_hbm = pl.BlockSpec(memory_space=pl.ANY)


def split(value):
    high = value.astype(jnp.bfloat16)
    low = (value - high.astype(jnp.float32)).astype(jnp.bfloat16)
    return high, low


def product(left, right, dims):
    def one(a, b):
        return lax.dot_general(a, b, dims, preferred_element_type=jnp.float32)

    return one(left[0], right[0]) + (one(left[0], right[1]) + one(left[1], right[0]))


def params(**more):
    return pltpu.CompilerParams(vmem_limit_bytes=VMEM_LIMIT, **more)


def prepare_kernel(linv, lower, uinv, upper, rhs, fmat, bmat, fall, ball, rhs_t):
    def maps(inverse, coupling, out):
        made = []
        for i in range(2):
            made.append(-product(split(inverse[i]), split(coupling[i]), NN))
            out[i] = made[i]
        return [split(m) for m in made]

    first, second = maps(linv, lower, fmat)
    fall[...] = product(second, first, NN)
    first, second = maps(uinv, upper, bmat)
    ball[...] = product(first, second, NN)
    for i in range(2):
        rhs_t[i] = rhs[i].T


def leaf_forward_kernel(targets, place, linv, rhs, low, fwd, *rest):
    outs, (acc, sems) = rest[:8], rest[8:]
    k = pl.program_id(0)
    core, z = place[0], place[1]

    @pl.when(k == 0)
    def _():
        def clear(i, carry):
            acc[i] = jnp.zeros(acc.shape[1:], jnp.float32)
            return carry

        lax.fori_loop(0, acc.shape[0], clear, 0)

    value = product(split(linv[0]), split(rhs[0]), NN)
    fwd[0] = value
    turned = split(value.T)
    for c in range(2):
        t = targets[2 * k + c]
        coupled = product(turned, split(low[0, c]), NT)
        for layer in range(LAYERS):
            side = lax.rem(layer % 2 + core, 2)
            away = lax.rem(layer // 2 - z + 4, 4)
            acc[(side * 4 + away) * TOPS + t] += coupled[layer * COLS : (layer + 1) * COLS]

    @pl.when(k == pl.num_programs(0) - 1)
    def _():
        copies = [
            pltpu.make_async_copy(acc.at[pl.ds(i * TOPS, TOPS)], outs[i], sems.at[i])
            for i in range(8)
        ]
        for copy in copies:
            copy.start()
        for copy in copies:
            copy.wait()


def leaf_forward(targets, place, linv, rhs, low):
    leaves = linv.shape[0]
    tile = pl.BlockSpec((1, TILE, TILE), lambda k, *_: (k, 0, 0))
    pair = pl.BlockSpec((1, 2, TILE, TILE), lambda k, *_: (k, 0, 0, 0))
    part = jax.ShapeDtypeStruct((TOPS, COLS, TILE), jnp.float32)
    return pl.pallas_call(
        leaf_forward_kernel,
        out_shape=[jax.ShapeDtypeStruct(linv.shape, jnp.float32)] + [part] * 8,
        grid_spec=pltpu.PrefetchScalarGridSpec(
            num_scalar_prefetch=2,
            grid=(leaves,),
            in_specs=[tile, tile, pair],
            out_specs=[tile] + [in_hbm] * 8,
            scratch_shapes=[
                pltpu.VMEM((8 * TOPS, COLS, TILE), jnp.float32),
                pltpu.SemaphoreType.DMA((8,)),
            ],
        ),
        compiler_params=params(),
        name="leaf_forward",
    )(targets, place, linv, rhs, low)


def enter_kernel(parts, rhs_t, linv, fmat, vec, spread):
    made = []
    for i in range(2):
        total = parts[0, i]
        for g in range(1, GRID):
            total = total + parts[g, i]
        made.append(product(split(rhs_t[i] - total), split(linv[i]), NT))
        vec[i] = made[i]
    last = made[1] + product(split(made[0]), split(fmat[1]), NT)
    for g in range(GRID):
        spread[g] = last


def turn_kernel(place, values, chain, vec, fmat, uinv, bmat, out, spread, states):
    states[0] = jnp.zeros(states.shape[1:], jnp.float32)
    states[1] = values[0]
    carried = values[0]
    for h in range(1, GRID - 1):
        carried = values[h] + product(split(carried), split(chain[h]), NT)
        states[h + 1] = carried
    incoming = states[place[2]]
    first = vec[0] + product(split(incoming), split(fmat[0]), NT)
    second = vec[1] + product(split(first), split(fmat[1]), NT)
    upper_second = product(split(second), split(uinv[1]), NT)
    upper_first = product(split(first), split(uinv[0]), NT)
    out[0] = upper_first
    out[1] = upper_second
    last = upper_first + product(split(upper_second), split(bmat[0]), NT)
    for g in range(GRID):
        spread[g] = last


def leave_kernel(place, values, chain, vec, bmat, out, states):
    states[GRID - 1] = jnp.zeros(states.shape[1:], jnp.float32)
    states[GRID - 2] = values[GRID - 1]
    carried = values[GRID - 1]
    for h in range(GRID - 2, 0, -1):
        carried = values[h] + product(split(carried), split(chain[h]), NT)
        states[h - 1] = carried
    incoming = states[place[2]]
    second = vec[1] + product(split(incoming), split(bmat[1]), NT)
    out[1] = second
    out[0] = vec[0] + product(split(second), split(bmat[0]), NT)


def leaf_back_kernel(targets, place, uinv, up, fwd, solved, out, own):
    k = pl.program_id(0)
    rest = fwd[0]
    for c in range(2):
        t = targets[2 * k + c]
        picked = solved[:, t].reshape(TILE, TILE)
        rest = rest - product(split(up[0, c]), split(picked), NT)
    out[0] = product(split(uinv[0]), split(rest), NN)

    @pl.when(k < 2)
    def _():
        own[k] = solved[:, 2 * place[2] + k].reshape(TILE, TILE).T


def leaf_back(targets, place, uinv, up, fwd, solved):
    leaves = uinv.shape[0]
    tile = pl.BlockSpec((1, TILE, TILE), lambda k, *_: (k, 0, 0))
    pair = pl.BlockSpec((1, 2, TILE, TILE), lambda k, *_: (k, 0, 0, 0))
    return pl.pallas_call(
        leaf_back_kernel,
        out_shape=[
            jax.ShapeDtypeStruct(uinv.shape, jnp.float32),
            jax.ShapeDtypeStruct((2, TILE, TILE), jnp.float32),
        ],
        grid_spec=pltpu.PrefetchScalarGridSpec(
            num_scalar_prefetch=2,
            grid=(leaves,),
            in_specs=[tile, pair, tile, whole],
            out_specs=[tile, pl.BlockSpec((2, TILE, TILE), lambda k, *_: (0, 0, 0))],
        ),
        compiler_params=params(),
        name="leaf_back",
    )(targets, place, uinv, up, fwd, solved)


def local(
    leaf_rhs,
    leaf_linv,
    leaf_uinv,
    low_couple,
    up_couple,
    targets,
    top_rhs,
    top_linv,
    top_uinv,
    top_lower,
    top_upper,
):
    layer, grid = lax.axis_index("layer"), lax.axis_index("grid")
    core, z = lax.rem(layer, 2), lax.div(layer, 2)
    place = jnp.stack([core, z, grid, layer]).astype(jnp.int32)
    flat = targets.reshape(-1)
    struct = jax.ShapeDtypeStruct
    square = struct((TILE, TILE), jnp.float32)
    two = struct((2, TILE, TILE), jnp.float32)
    slim = struct((2, COLS, TILE), jnp.float32)
    spread = struct((GRID, COLS, TILE), jnp.float32)
    smem = pl.BlockSpec(memory_space=pltpu.SMEM)

    fmat, bmat, fall, ball, rhs_t = pl.pallas_call(
        prepare_kernel,
        out_shape=[two, two, square, square, two],
        in_specs=[whole] * 5,
        out_specs=[whole] * 5,
        compiler_params=params(),
        name="prepare",
    )(top_linv, top_lower, top_uinv, top_upper, top_rhs)
    fchain = lax.all_gather(fall, "grid", axis=0, tiled=False)
    bchain = lax.all_gather(ball, "grid", axis=0, tiled=False)

    fwd, *parts = leaf_forward(flat, place, leaf_linv, leaf_rhs, low_couple)
    other = [(i, i + 1 - 2 * (i % 2)) for i in range(LAYERS)]
    sums = [parts[d] + lax.ppermute(parts[4 + d], "layer", other) for d in range(4)]

    def along_z(value, d):
        return lax.ppermute(value, "layer", [(i, (i + 2 * d) % LAYERS) for i in range(LAYERS)])

    total = sums[0] + along_z(sums[1], 1) + along_z(sums[2], 2) + along_z(sums[3], 3)
    arrived = lax.all_to_all(
        total.reshape(GRID * 2, COLS, TILE), "grid", split_axis=0, concat_axis=0, tiled=True
    ).reshape(GRID, 2, COLS, TILE)

    mine = pl.BlockSpec((2, COLS, TILE), lambda i, where: (0, where[3], 0))

    def plain(shape):
        return pl.BlockSpec(shape, lambda i, where: (0,) * len(shape))

    def enter(where, *refs):
        enter_kernel(*refs)

    vec, sent = pl.pallas_call(
        enter,
        out_shape=[slim, spread],
        grid_spec=pltpu.PrefetchScalarGridSpec(
            num_scalar_prefetch=1,
            grid=(1,),
            in_specs=[
                plain((GRID, 2, COLS, TILE)),
                mine,
                plain((2, TILE, TILE)),
                plain((2, TILE, TILE)),
            ],
            out_specs=[plain((2, COLS, TILE)), plain((GRID, COLS, TILE))],
        ),
        compiler_params=params(),
        name="enter",
    )(place, arrived, rhs_t, top_linv, fmat)

    values = lax.all_to_all(sent, "grid", split_axis=0, concat_axis=0, tiled=True)
    states = pltpu.VMEM((GRID, COLS, TILE), jnp.float32)
    upper_vec, sent_back = pl.pallas_call(
        turn_kernel,
        out_shape=[slim, spread],
        in_specs=[smem] + [whole] * 6,
        out_specs=[whole] * 2,
        scratch_shapes=[states],
        compiler_params=params(),
        name="turn",
    )(place, values, fchain, vec, fmat, top_uinv, bmat)

    values_back = lax.all_to_all(sent_back, "grid", split_axis=0, concat_axis=0, tiled=True)
    sol_t = pl.pallas_call(
        leave_kernel,
        out_shape=slim,
        in_specs=[smem] + [whole] * 4,
        out_specs=whole,
        scratch_shapes=[states],
        compiler_params=params(),
        name="leave",
    )(place, values_back, bchain, upper_vec, bmat)

    solved = lax.all_gather(sol_t, ("layer", "grid"), axis=0, tiled=True)
    solved = solved.reshape(LAYERS, TOPS, COLS, TILE)
    return tuple(leaf_back(flat, place, leaf_uinv, up_couple, fwd, solved))


def solution(mesh):
    leaf = P(("layer", "grid"), None, None)
    leaf_pair = P(("layer", "grid"), None, None, None)
    top = P("grid", None, None)
    return jax.shard_map(
        local,
        mesh=mesh,
        in_specs=(leaf, leaf, leaf, leaf_pair, leaf_pair, P(("layer", "grid"), None))
        + (top,) * 5,
        out_specs=(leaf, top),
        check_vma=False,
    )
```

```python
import jax
import jax.numpy as jnp
from jax import lax
from jax.experimental import pallas as pl
from jax.experimental.pallas import tpu as pltpu
from jax.sharding import PartitionSpec as P

LAYERS = 8
GRID = 16
TILE = 256
COLS = TILE // LAYERS
TOPS = 32
MIB = 1024 * 1024
HALF = TILE // 2

NN = (((1,), (0,)), ((), ()))
NT = (((1,), (1,)), ((), ()))

whole = pl.BlockSpec(memory_space=pltpu.VMEM)
in_hbm = pl.BlockSpec(memory_space=pl.ANY)


def split(value):
    high = value.astype(jnp.bfloat16)
    low = (value - high.astype(jnp.float32)).astype(jnp.bfloat16)
    return high, low


def product(left, right, dims):
    ((near,), (far,)), _ = dims
    wide = jnp.concatenate([left[0], left[0], left[1]], axis=near)
    tall = jnp.concatenate([right[0], right[1], right[0]], axis=far)
    return lax.dot_general(wide, tall, dims, preferred_element_type=jnp.float32)


def params(mib):
    return pltpu.CompilerParams(vmem_limit_bytes=mib * MIB)


def prepare_kernel(linv, lower, uinv, upper, rhs, fmat, bmat, share, rhs_t):
    core = lax.rem(lax.axis_index("layer"), 2)
    rows = pl.ds(pl.multiple_of(core * HALF, HALF), HALF)

    def maps(inverse, coupling, out):
        for i in range(2):
            out[i] = -product(split(inverse[i]), split(coupling[i]), NN)

    maps(linv, lower, fmat)
    share[0] = product(split(fmat[1, rows]), split(fmat[0]), NN)
    maps(uinv, upper, bmat)
    share[1] = product(split(bmat[0, rows]), split(bmat[1]), NN)
    for i in range(2):
        rhs_t[i] = rhs[i].T


def leaf_forward_kernel(targets, linv, rhs, low, fwd, *rest):
    outs, (acc, sems) = rest[:10], rest[10:]
    k = pl.program_id(0)
    layer = lax.axis_index("layer")
    core, z = lax.rem(layer, 2), lax.div(layer, 2)

    @pl.when(k == 0)
    def _():
        def clear(i, carry):
            acc[i] = jnp.zeros(acc.shape[1:], jnp.float32)
            return carry

        lax.fori_loop(0, acc.shape[0], clear, 0, unroll=8)

    leaves = linv.shape[0]
    turned = []
    for leaf in range(leaves):
        value = product(split(linv[leaf]), split(rhs[leaf]), NN)
        fwd[leaf] = value
        turned.append(split(value.T))
    for leaf in range(leaves):
        for c in range(2):
            t = targets[k * leaves + leaf, c]
            owner, odd = lax.div(t, 2), lax.rem(t, 2)
            coupled = product(turned[leaf], split(low[leaf, c]), NT)
            for goal in range(LAYERS):
                side = lax.rem(goal % 2 + core, 2)
                away = lax.rem(goal // 2 - z + 4, 4)
                even_place = (side * 4 + away) * GRID + owner
                odd_place = 8 * GRID + (side * GRID + owner) * 4 + away
                acc[jnp.where(odd == 0, even_place, odd_place)] += coupled[
                    goal * COLS : (goal + 1) * COLS
                ]

    @pl.when(k == pl.num_programs(0) - 1)
    def _():
        copies, start = [], 0
        for i, out in enumerate(outs):
            size = out.shape[0]
            copies.append(pltpu.make_async_copy(acc.at[pl.ds(start, size)], out, sems.at[i]))
            start += size
        for copy in copies:
            copy.start()
        for copy in copies:
            copy.wait()


def leaf_forward(targets, linv, rhs, low, step=2):
    leaves = linv.shape[0]
    tile = pl.BlockSpec((step, TILE, TILE), lambda k, *_: (k, 0, 0))
    pair = pl.BlockSpec((step, 2, TILE, TILE), lambda k, *_: (k, 0, 0, 0))
    even = jax.ShapeDtypeStruct((GRID, COLS, TILE), jnp.float32)
    odd = jax.ShapeDtypeStruct((GRID * 4, COLS, TILE), jnp.float32)
    return pl.pallas_call(
        leaf_forward_kernel,
        out_shape=[jax.ShapeDtypeStruct(linv.shape, jnp.float32)] + [even] * 8 + [odd] * 2,
        grid_spec=pltpu.PrefetchScalarGridSpec(
            num_scalar_prefetch=1,
            grid=(leaves // step,),
            in_specs=[tile, tile, pair],
            out_specs=[tile] + [pl.BlockSpec(memory_space=pltpu.HBM)] * 10,
            scratch_shapes=[
                pltpu.VMEM((16 * GRID, COLS, TILE), jnp.float32),
                pltpu.SemaphoreType.DMA((10,)),
            ],
        ),
        compiler_params=params(56),
        name="leaf_forward",
    )(targets, linv, rhs, low)


def fold_kernel(parts, *outs):
    for i, out in enumerate(outs):
        total = parts[0, i]
        for g in range(1, GRID):
            total = total + parts[g, i]
        out[...] = total


def enter_kernel(even, odd, odd_1, odd_2, odd_3, rhs_t, linv, fmat, vec, spread):
    rows = pl.ds(pl.multiple_of(lax.axis_index("layer") * COLS, COLS), COLS)
    total = even[0]
    for g in range(1, GRID):
        total = total + even[g]
    first = product(split(rhs_t[0, rows] - total), split(linv[0]), NT)
    total = (odd[...] + odd_1[...]) + (odd_2[...] + odd_3[...])
    second = product(split(rhs_t[1, rows] - total), split(linv[1]), NT)
    vec[0] = first
    vec[1] = second
    last = second + product(split(first), split(fmat[1]), NT)
    for g in range(GRID):
        spread[g] = last


def chain_kernel(own, other, forward, backward):
    core = lax.rem(lax.axis_index("layer"), 2)
    for i, source in enumerate((own, other)):
        side = core if i == 0 else 1 - core
        rows = pl.ds(pl.multiple_of(side * HALF, HALF), HALF)
        for h in range(1, GRID - 1):
            for which, out in enumerate((forward, backward)):
                high, low = split(source[2 * h + which])
                out[0, h, rows] = high
                out[1, h, rows] = low


def chain_pairs(own, other):
    pairs = jax.ShapeDtypeStruct((2, GRID, TILE, TILE), jnp.bfloat16)
    return pl.pallas_call(
        chain_kernel,
        out_shape=[pairs, pairs],
        in_specs=[whole] * 2,
        out_specs=[whole] * 2,
        compiler_params=params(20),
        name="chain_pairs",
    )(own, other)


def turn_kernel(values, chain, vec, fmat, uinv, bmat, out, spread, states):
    states[0] = jnp.zeros(states.shape[1:], jnp.float32)
    states[1] = values[0]
    carried = values[0]
    for h in range(1, GRID - 1):
        carried = values[h] + product(split(carried), (chain[0, h], chain[1, h]), NT)
        states[h + 1] = carried
    incoming = states[lax.axis_index("grid")]
    first = vec[0] + product(split(incoming), split(fmat[0]), NT)
    second = vec[1] + product(split(first), split(fmat[1]), NT)
    upper_second = product(split(second), split(uinv[1]), NT)
    upper_first = product(split(first), split(uinv[0]), NT)
    out[0] = upper_first
    out[1] = upper_second
    last = upper_first + product(split(upper_second), split(bmat[0]), NT)
    for g in range(GRID):
        spread[g] = last


def leave_kernel(values, chain, vec, bmat, even, spread, states):
    states[GRID - 1] = jnp.zeros(states.shape[1:], jnp.float32)
    states[GRID - 2] = values[GRID - 1]
    carried = values[GRID - 1]
    for h in range(GRID - 2, 0, -1):
        carried = values[h] + product(split(carried), (chain[0, h], chain[1, h]), NT)
        states[h - 1] = carried
    incoming = states[lax.axis_index("grid")]
    second = vec[1] + product(split(incoming), split(bmat[1]), NT)
    even[...] = vec[0] + product(split(second), split(bmat[0]), NT)
    for g in range(GRID):
        spread[g] = second


def copies_kernel(first, second, third, fourth, spread):
    for g in range(GRID):
        for d, value in enumerate((first, second, third, fourth)):
            spread[g, d] = value[...]


def leaf_ready_kernel(uinv, up, fwd, base, factor):
    for leaf in range(uinv.shape[0]):
        inverse = split(uinv[leaf])
        base[leaf] = product(inverse, split(fwd[leaf]), NN)
        for c in range(2):
            factor[leaf, c] = product(inverse, split(up[leaf, c]), NN)


def leaf_ready(uinv, up, fwd, step=2):
    tile = pl.BlockSpec((step, TILE, TILE), lambda k: (k, 0, 0))
    pair = pl.BlockSpec((step, 2, TILE, TILE), lambda k: (k, 0, 0, 0))
    return pl.pallas_call(
        leaf_ready_kernel,
        out_shape=[jax.ShapeDtypeStruct(x.shape, jnp.float32) for x in (uinv, up)],
        grid=(uinv.shape[0] // step,),
        in_specs=[tile, pair, tile],
        out_specs=[tile, pair],
        compiler_params=params(20),
        name="leaf_ready",
    )(uinv, up, fwd)


def leaf_back_kernel(targets, base, factor, *rest):
    even, odd, (out, own, solved, sems) = rest[:2], rest[2], rest[3:]
    k = pl.program_id(0)
    leaves = base.shape[0]
    layer = lax.axis_index("layer")
    core, z = lax.rem(layer, 2), lax.div(layer, 2)

    @pl.when(k == 0)
    def _():
        copies = []
        for side in range(2):
            for d in range(4):
                place = 2 * lax.rem(z - d + 4, 4) + (core if side == 0 else 1 - core)
                for i, source in enumerate((even[side].at[:, d], odd.at[place])):
                    copies.append(
                        pltpu.make_async_copy(
                            source, solved.at[i, :, place], sems.at[i, side * 4 + d]
                        )
                    )
        for copy in copies:
            copy.start()
        for copy in copies:
            copy.wait()
        for i in range(2):
            own[i] = solved[i, lax.axis_index("grid")].reshape(TILE, TILE).T

    for leaf in range(leaves):
        value = base[leaf]
        for c in range(2):
            t = targets[k * leaves + leaf, c]
            picked = solved[lax.rem(t, 2), lax.div(t, 2)].reshape(TILE, TILE)
            value = value - product(split(factor[leaf, c]), split(picked), NT)
        out[leaf] = value


def leaf_back(targets, base, factor, even, odd, step=2):
    leaves = base.shape[0]
    tile = pl.BlockSpec((step, TILE, TILE), lambda k, *_: (k, 0, 0))
    pair = pl.BlockSpec((step, 2, TILE, TILE), lambda k, *_: (k, 0, 0, 0))
    return pl.pallas_call(
        leaf_back_kernel,
        out_shape=[
            jax.ShapeDtypeStruct(base.shape, jnp.float32),
            jax.ShapeDtypeStruct((2, TILE, TILE), jnp.float32),
        ],
        grid_spec=pltpu.PrefetchScalarGridSpec(
            num_scalar_prefetch=1,
            grid=(leaves // step,),
            in_specs=[tile, pair] + [in_hbm] * 3,
            out_specs=[tile, pl.BlockSpec((2, TILE, TILE), lambda k, *_: (0, 0, 0))],
            scratch_shapes=[
                pltpu.VMEM((2, GRID, LAYERS, COLS, TILE), jnp.float32),
                pltpu.SemaphoreType.DMA((2, 8)),
            ],
        ),
        compiler_params=params(56),
        name="leaf_back",
    )(targets, base, factor, *even, odd)


def call(kernel, outs, name, *args, scratch=(), mib=10):
    return pl.pallas_call(
        kernel,
        out_shape=[jax.ShapeDtypeStruct(shape, jnp.float32) for shape in outs],
        in_specs=[whole] * len(args),
        out_specs=[whole] * len(outs),
        scratch_shapes=list(scratch),
        compiler_params=params(mib),
        name=name,
    )(*args)


def after(values):
    return lax.optimization_barrier(values)


def other_core(value):
    return lax.ppermute(value, "layer", [(i, i + 1 - 2 * (i % 2)) for i in range(LAYERS)])


def along_z(value, steps):
    return lax.ppermute(value, "layer", [(i, (i + 2 * steps) % LAYERS) for i in range(LAYERS)])


def exchange(value):
    return lax.all_to_all(value, "grid", split_axis=0, concat_axis=0, tiled=True)


def local(
    leaf_rhs,
    leaf_linv,
    leaf_uinv,
    low_couple,
    up_couple,
    targets,
    top_rhs,
    top_linv,
    top_uinv,
    top_lower,
    top_upper,
):
    two = (2, TILE, TILE)
    slim = (2, COLS, TILE)
    piece = (COLS, TILE)
    spread = (GRID, COLS, TILE)

    tops = (top_linv, top_lower, top_uinv, top_upper, top_rhs)
    fmat, bmat, share, rhs_t = call(
        prepare_kernel, [two, two, (2, HALF, TILE), two], "prepare", *tops, mib=56
    )
    share, leaf_rhs = after((share, leaf_rhs))
    chain = lax.all_gather(share, "grid", axis=0, tiled=True)
    fwd, *parts = leaf_forward(targets, leaf_linv, leaf_rhs, low_couple)
    even_keep, even_send, odd_keep, odd_send = parts[:4], parts[4:8], parts[8], parts[9]
    even = [even_keep[d] + other_core(even_send[d]) for d in (1, 2, 3, 0)]
    odd = odd_keep + other_core(odd_send)
    even = even[3] + along_z(even[0], 1) + along_z(even[1], 2) + along_z(even[2], 3)
    odd = exchange(odd).reshape(GRID, 4, COLS, TILE)
    even, odd = after((even, odd))
    odd = call(fold_kernel, [piece] * 4, "fold", odd)
    odd = [odd[0]] + [along_z(odd[d], d) for d in range(1, 4)]
    even = exchange(even)

    vec, sent = call(
        enter_kernel, [slim, spread], "enter", even, *odd, rhs_t, tops[0], fmat
    )
    vec, sent, chain = after((vec, sent, chain))
    forward, backward = chain_pairs(chain, other_core(chain))
    values = exchange(sent)
    values, forward, backward = after((values, forward, backward))
    states = [pltpu.VMEM(spread, jnp.float32)]
    vec, sent = call(
        turn_kernel,
        [slim, spread],
        "turn",
        *(values, forward, vec, fmat, tops[2], bmat),
        scratch=states,
        mib=56,
    )
    sent, leaf_uinv = after((sent, leaf_uinv))
    values = exchange(sent)
    base, factor = leaf_ready(leaf_uinv, up_couple, fwd)
    values, base, factor = after((values, base, factor))
    even, sent = call(
        leave_kernel,
        [piece, spread],
        "leave",
        *(values, backward, vec, bmat),
        scratch=states,
        mib=56,
    )
    even = [even] + [along_z(even, d) for d in range(1, 4)]
    [even] = call(copies_kernel, [(GRID, 4, COLS, TILE)], "copies", *even)
    odd = exchange(sent)
    even, odd = after((even, odd))
    odd = lax.all_gather(odd, "layer", axis=0, tiled=False)
    even = exchange(even.reshape(GRID * 4, COLS, TILE)).reshape(GRID, 4, COLS, TILE)
    even = [even, other_core(even)]
    return tuple(leaf_back(targets, base, factor, even, odd))


def solution(mesh):
    leaf = P(("layer", "grid"), None, None)
    leaf_pair = P(("layer", "grid"), None, None, None)
    top = P("grid", None, None)
    return jax.shard_map(
        local,
        mesh=mesh,
        in_specs=(leaf, leaf, leaf, leaf_pair, leaf_pair, P(("layer", "grid"), None))
        + (top,) * 5,
        out_specs=(leaf, top),
        check_vma=False,
    )
```

```python
import jax
import jax.numpy as jnp
from jax import lax
from jax.experimental import pallas as pl
from jax.experimental.pallas import tpu as pltpu
from jax.sharding import PartitionSpec as P

LAYERS = 8
GRID = 16
TILE = 256
COLS = TILE // LAYERS
TOPS = 32
MIB = 1024 * 1024
HALF = TILE // 2

NN = (((1,), (0,)), ((), ()))
NT = (((1,), (1,)), ((), ()))

whole = pl.BlockSpec(memory_space=pltpu.VMEM)
in_hbm = pl.BlockSpec(memory_space=pl.ANY)


def split(value):
    high = value.astype(jnp.bfloat16)
    low = (value - high.astype(jnp.float32)).astype(jnp.bfloat16)
    return high, low


def product(left, right, dims):
    ((near,), (far,)), _ = dims
    wide = jnp.concatenate([left[0], left[0], left[1]], axis=near)
    tall = jnp.concatenate([right[0], right[1], right[0]], axis=far)
    return lax.dot_general(wide, tall, dims, preferred_element_type=jnp.float32)


far = pl.BlockSpec(memory_space=pltpu.HBM)


def params(mib):
    return pltpu.CompilerParams(vmem_limit_bytes=mib * MIB)


def cost(flops):
    return pl.CostEstimate(flops=flops, bytes_accessed=0, transcendentals=0)


def prepare_kernel(linv, lower, uinv, upper, rhs, fmat, bmat, share, rhs_t):
    core = lax.rem(lax.axis_index("layer"), 2)
    rows = pl.ds(pl.multiple_of(core * HALF, HALF), HALF)

    def maps(inverse, coupling, out):
        for i in range(2):
            out[i] = -product(split(inverse[i]), split(coupling[i]), NN)

    maps(linv, lower, fmat)
    share[0] = product(split(fmat[1, rows]), split(fmat[0]), NN)
    maps(uinv, upper, bmat)
    share[1] = product(split(bmat[0, rows]), split(bmat[1]), NN)
    for i in range(2):
        rhs_t[i] = rhs[i].T


def leaf_forward_kernel(targets, linv, rhs, low, fwd, *rest):
    outs, (acc, linv_in, rhs_in, low_in, fwd_out, in_sems, fwd_sems, sems) = rest[:10], rest[10:]
    leaves = linv.shape[0]
    layer = lax.axis_index("layer")
    core, z = lax.rem(layer, 2), lax.div(layer, 2)
    reads = [
        [
            pltpu.make_async_copy(source.at[k], held.at[k], in_sems.at[i, k])
            for i, (source, held) in enumerate(((linv, linv_in), (rhs, rhs_in), (low, low_in)))
        ]
        for k in range(leaves)
    ]
    for group in reads:
        for copy in group:
            copy.start()

    def clear(i, carry):
        acc[i] = jnp.zeros(acc.shape[1:], jnp.float32)
        return carry

    lax.fori_loop(0, acc.shape[0], clear, 0, unroll=8)
    writes = []
    for start in range(0, leaves, 2):
        pair = range(start, start + 2)
        for k in pair:
            for copy in reads[k]:
                copy.wait()
        turned = []
        for k in pair:
            value = product(split(linv_in[k]), split(rhs_in[k]), NN)
            fwd_out[k] = value
            turned.append(split(value.T))
        for k in pair:
            for c in range(2):
                t = targets[k, c]
                owner, odd = lax.div(t, 2), lax.rem(t, 2)
                coupled = product(turned[k - start], split(low_in[k, c]), NT)
                for goal in range(LAYERS):
                    side = lax.rem(goal % 2 + core, 2)
                    away = lax.rem(goal // 2 - z + 4, 4)
                    even_place = (side * 4 + away) * GRID + owner
                    odd_place = 8 * GRID + (side * GRID + owner) * 4 + away
                    acc[jnp.where(odd == 0, even_place, odd_place)] += coupled[
                        goal * COLS : (goal + 1) * COLS
                    ]
        for k in pair:
            writes.append(pltpu.make_async_copy(fwd_out.at[k], fwd.at[k], fwd_sems.at[k]))
            writes[-1].start()
    place = 0
    for i, out in enumerate(outs):
        size = out.shape[0]
        writes.append(pltpu.make_async_copy(acc.at[pl.ds(place, size)], out, sems.at[i]))
        writes[-1].start()
        place += size
    for copy in writes:
        copy.wait()


def leaf_forward(targets, linv, rhs, low):
    leaves = linv.shape[0]
    even = jax.ShapeDtypeStruct((GRID, COLS, TILE), jnp.float32)
    odd = jax.ShapeDtypeStruct((GRID * 4, COLS, TILE), jnp.float32)
    return pl.pallas_call(
        leaf_forward_kernel,
        out_shape=[jax.ShapeDtypeStruct(linv.shape, jnp.float32)] + [even] * 8 + [odd] * 2,
        in_specs=[pl.BlockSpec(memory_space=pltpu.SMEM)] + [far] * 3,
        out_specs=[far] * 11,
        scratch_shapes=[
            pltpu.VMEM((16 * GRID, COLS, TILE), jnp.float32),
            pltpu.VMEM(linv.shape, jnp.float32),
            pltpu.VMEM(rhs.shape, jnp.float32),
            pltpu.VMEM(low.shape, jnp.float32),
            pltpu.VMEM(linv.shape, jnp.float32),
            pltpu.SemaphoreType.DMA((3, leaves)),
            pltpu.SemaphoreType.DMA((leaves,)),
            pltpu.SemaphoreType.DMA((10,)),
        ],
        compiler_params=params(58),
        name="leaf_forward",
    )(targets, linv, rhs, low)


def gathered_kernel(first, second, third, fourth, out):
    out[...] = (first[...] + second[...]) + (third[...] + fourth[...])


def fold_kernel(parts, *outs):
    for i, out in enumerate(outs):
        total = parts[0, i]
        for g in range(1, GRID):
            total = total + parts[g, i]
        out[...] = total


def enter_kernel(even, odd, odd_1, odd_2, odd_3, rhs_t, linv, fmat, vec, spread):
    rows = pl.ds(pl.multiple_of(lax.axis_index("layer") * COLS, COLS), COLS)
    total = even[0]
    for g in range(1, GRID):
        total = total + even[g]
    first = product(split(rhs_t[0, rows] - total), split(linv[0]), NT)
    total = (odd[...] + odd_1[...]) + (odd_2[...] + odd_3[...])
    second = product(split(rhs_t[1, rows] - total), split(linv[1]), NT)
    vec[0] = first
    vec[1] = second
    last = second + product(split(first), split(fmat[1]), NT)
    for g in range(GRID):
        spread[g] = last


def chain_kernel(own, other, forward, backward):
    core = lax.rem(lax.axis_index("layer"), 2)
    for i, source in enumerate((own, other)):
        side = core if i == 0 else 1 - core
        rows = pl.ds(pl.multiple_of(side * HALF, HALF), HALF)
        for h in range(1, GRID - 1):
            for which, out in enumerate((forward, backward)):
                high, low = split(source[2 * h + which])
                out[0, h, rows] = high
                out[1, h, rows] = low


def chain_pairs(own, other):
    pairs = jax.ShapeDtypeStruct((2, GRID, TILE, TILE), jnp.bfloat16)
    return pl.pallas_call(
        chain_kernel,
        out_shape=[pairs, pairs],
        in_specs=[whole] * 2,
        out_specs=[whole] * 2,
        compiler_params=params(20),
        name="chain_pairs",
    )(own, other)


def turn_kernel(values, chain, vec, fmat, uinv, bmat, out, spread, states):
    states[0] = jnp.zeros(states.shape[1:], jnp.float32)
    states[1] = values[0]
    carried = values[0]
    for h in range(1, GRID - 1):
        carried = values[h] + product(split(carried), (chain[0, h], chain[1, h]), NT)
        states[h + 1] = carried
    incoming = states[lax.axis_index("grid")]
    first = vec[0] + product(split(incoming), split(fmat[0]), NT)
    second = vec[1] + product(split(first), split(fmat[1]), NT)
    upper_second = product(split(second), split(uinv[1]), NT)
    upper_first = product(split(first), split(uinv[0]), NT)
    out[0] = upper_first
    out[1] = upper_second
    last = upper_first + product(split(upper_second), split(bmat[0]), NT)
    for g in range(GRID):
        spread[g] = last


def leave_kernel(values, chain, vec, bmat, even, spread, states):
    states[GRID - 1] = jnp.zeros(states.shape[1:], jnp.float32)
    states[GRID - 2] = values[GRID - 1]
    carried = values[GRID - 1]
    for h in range(GRID - 2, 0, -1):
        carried = values[h] + product(split(carried), (chain[0, h], chain[1, h]), NT)
        states[h - 1] = carried
    incoming = states[lax.axis_index("grid")]
    second = vec[1] + product(split(incoming), split(bmat[1]), NT)
    even[...] = vec[0] + product(split(second), split(bmat[0]), NT)
    for g in range(GRID):
        spread[g] = second


def copies_kernel(first, second, third, fourth, spread):
    z = lax.div(lax.axis_index("layer"), 2)
    for d, value in enumerate((first, second, third, fourth)):
        for g in range(GRID):
            spread[g, lax.rem(z - d + 4, 4)] = value[...]


def leaf_ready_kernel(uinv, up, fwd, base, factor):
    for leaf in range(uinv.shape[0]):
        inverse = split(uinv[leaf])
        base[leaf] = product(inverse, split(fwd[leaf]), NN)
        for c in range(2):
            factor[leaf, c] = product(inverse, split(up[leaf, c]), NN)


def leaf_ready(uinv, up, fwd, step=2):
    tile = pl.BlockSpec((step, TILE, TILE), lambda k: (k, 0, 0))
    pair = pl.BlockSpec((step, 2, TILE, TILE), lambda k: (k, 0, 0, 0))
    return pl.pallas_call(
        leaf_ready_kernel,
        out_shape=[jax.ShapeDtypeStruct(x.shape, jnp.float32) for x in (uinv, up)],
        grid=(uinv.shape[0] // step,),
        in_specs=[tile, pair, tile],
        out_specs=[tile, pair],
        compiler_params=params(20),
        name="leaf_ready",
    )(uinv, up, fwd)


def leaf_back_kernel(
    targets, base, factor, even, even_other, odd, out, own,
    solved, base_in, factor_in, out_held, own_held, sems, in_sems, out_sems,
):
    leaves = base.shape[0]
    core = lax.rem(lax.axis_index("layer"), 2)

    def read(slot, t):
        owner = lax.div(t, 2)

        @pl.when(lax.rem(t, 2) == 1)
        def _():
            pltpu.make_async_copy(odd.at[:, :, owner], solved.at[slot], sems.at[slot]).start()

        @pl.when(lax.rem(t, 2) == 0)
        def _():
            for source, side in ((even, core), (even_other, 1 - core)):
                pltpu.make_async_copy(
                    source.at[owner], solved.at[slot, :, side], sems.at[slot]
                ).start()

    def ready(slot):
        pltpu.make_async_copy(odd.at[:, :, 0], solved.at[slot], sems.at[slot]).wait()

    reads = []
    for k in range(leaves):
        for c in range(2):
            read(2 * k + c, targets[k, c])
        reads.append(
            [
                pltpu.make_async_copy(base.at[k], base_in.at[k], in_sems.at[0, k]),
                pltpu.make_async_copy(factor.at[k], factor_in.at[k], in_sems.at[1, k]),
            ]
        )
        for copy in reads[k]:
            copy.start()
    for i in range(2):
        read(2 * leaves + i, 2 * lax.axis_index("grid") + i)

    writes = []
    for start in range(0, leaves, 2):
        pair = range(start, start + 2)
        for k in pair:
            for copy in reads[k]:
                copy.wait()
            for c in range(2):
                ready(2 * k + c)
        for k in pair:
            value = base_in[k]
            for c in range(2):
                picked = solved[2 * k + c].reshape(TILE, TILE)
                value = value - product(split(factor_in[k, c]), split(picked), NT)
            out_held[k] = value
        for k in pair:
            writes.append(pltpu.make_async_copy(out_held.at[k], out.at[k], out_sems.at[k]))
            writes[-1].start()
    for i in range(2):
        ready(2 * leaves + i)
        own_held[i] = solved[2 * leaves + i].reshape(TILE, TILE).T
    writes.append(pltpu.make_async_copy(own_held, own, out_sems.at[leaves]))
    writes[-1].start()
    for copy in writes:
        copy.wait()


def leaf_back(targets, base, factor, even, odd):
    leaves = base.shape[0]
    two = (2, TILE, TILE)
    return pl.pallas_call(
        leaf_back_kernel,
        out_shape=[
            jax.ShapeDtypeStruct(base.shape, jnp.float32),
            jax.ShapeDtypeStruct(two, jnp.float32),
        ],
        in_specs=[pl.BlockSpec(memory_space=pltpu.SMEM)] + [far] * 2 + [in_hbm] * 2 + [far],
        out_specs=[far] * 2,
        scratch_shapes=[
            pltpu.VMEM((2 * leaves + 2, 4, 2, COLS, TILE), jnp.float32),
            pltpu.VMEM(base.shape, jnp.float32),
            pltpu.VMEM(factor.shape, jnp.float32),
            pltpu.VMEM(base.shape, jnp.float32),
            pltpu.VMEM(two, jnp.float32),
            pltpu.SemaphoreType.DMA((2 * leaves + 2,)),
            pltpu.SemaphoreType.DMA((2, leaves)),
            pltpu.SemaphoreType.DMA((leaves + 1,)),
        ],
        compiler_params=params(58),
        name="leaf_back",
    )(targets, base, factor, *even, odd)


def call(kernel, outs, name, *args, scratch=(), mib=10, hint=1_000_000):
    return pl.pallas_call(
        kernel,
        out_shape=[jax.ShapeDtypeStruct(shape, jnp.float32) for shape in outs],
        in_specs=[whole] * len(args),
        out_specs=[whole] * len(outs),
        scratch_shapes=list(scratch),
        compiler_params=params(mib),
        cost_estimate=cost(hint),
        name=name,
    )(*args)


def after(values):
    return lax.optimization_barrier(values)


def other_core(value):
    return lax.ppermute(value, "layer", [(i, i + 1 - 2 * (i % 2)) for i in range(LAYERS)])


def along_z(value, steps):
    return lax.ppermute(value, "layer", [(i, (i + 2 * steps) % LAYERS) for i in range(LAYERS)])


def exchange(value):
    return lax.all_to_all(value, "grid", split_axis=0, concat_axis=0, tiled=True)


def local(
    leaf_rhs,
    leaf_linv,
    leaf_uinv,
    low_couple,
    up_couple,
    targets,
    top_rhs,
    top_linv,
    top_uinv,
    top_lower,
    top_upper,
):
    two = (2, TILE, TILE)
    slim = (2, COLS, TILE)
    piece = (COLS, TILE)
    spread = (GRID, COLS, TILE)

    tops = (top_linv, top_lower, top_uinv, top_upper, top_rhs)
    fmat, bmat, share, rhs_t = call(
        prepare_kernel, [two, two, (2, HALF, TILE), two], "prepare", *tops, mib=56
    )
    share, leaf_rhs = after((share, leaf_rhs))
    chain = lax.all_gather(share, "grid", axis=0, tiled=True)
    fwd, *parts = leaf_forward(targets, leaf_linv, leaf_rhs, low_couple)
    even_keep, even_send, odd_keep, odd_send = parts[:4], parts[4:8], parts[8], parts[9]
    even = [even_keep[d] + other_core(even_send[d]) for d in (1, 2, 3, 0)]
    odd = odd_keep + other_core(odd_send)
    odd, leaf_uinv = after((odd, leaf_uinv))
    odd = exchange(odd).reshape(GRID, 4, COLS, TILE)
    base, factor = leaf_ready(leaf_uinv, up_couple, fwd)
    even = [even[3]] + [along_z(even[d - 1], d) for d in range(1, 4)]
    [even] = call(gathered_kernel, [spread], "gathered", *even)
    even, base, factor = after((even, base, factor))
    even, odd = after((even, odd))
    odd = call(fold_kernel, [piece] * 4, "fold", odd)
    odd = [odd[0]] + [along_z(odd[d], d) for d in range(1, 4)]
    even = exchange(even)

    vec, sent = call(
        enter_kernel, [slim, spread], "enter", even, *odd, rhs_t, tops[0], fmat
    )
    vec, sent, chain = after((vec, sent, chain))
    forward, backward = chain_pairs(chain, other_core(chain))
    values = exchange(sent)
    values, forward, backward = after((values, forward, backward))
    states = [pltpu.VMEM(spread, jnp.float32)]
    vec, sent = call(
        turn_kernel,
        [slim, spread],
        "turn",
        *(values, forward, vec, fmat, tops[2], bmat),
        scratch=states,
        mib=10,
    )
    values = exchange(sent)
    even, sent = call(
        leave_kernel,
        [piece, spread],
        "leave",
        *(values, backward, vec, bmat),
        scratch=states,
        mib=10,
    )
    even = [even] + [along_z(even, d) for d in range(1, 4)]
    [even] = call(copies_kernel, [(GRID, 4, COLS, TILE)], "copies", *even)
    odd = exchange(sent)
    even, odd = after((even, odd))
    odd = lax.all_gather(odd, "layer", axis=0, tiled=False).reshape(4, 2, *spread)
    even = exchange(even.reshape(GRID * 4, COLS, TILE)).reshape(GRID, 4, COLS, TILE)
    even = [even, other_core(even)]
    return tuple(leaf_back(targets, base, factor, even, odd))


def solution(mesh):
    leaf = P(("layer", "grid"), None, None)
    leaf_pair = P(("layer", "grid"), None, None, None)
    top = P("grid", None, None)
    return jax.shard_map(
        local,
        mesh=mesh,
        in_specs=(leaf, leaf, leaf, leaf_pair, leaf_pair, P(("layer", "grid"), None))
        + (top,) * 5,
        out_specs=(leaf, top),
        check_vma=False,
    )
```

```python
import functools

import jax
import jax.numpy as jnp
from jax import lax
from jax.experimental import pallas as pl
from jax.experimental.pallas import tpu as pltpu
from jax.sharding import PartitionSpec as P

LAYERS = 8
GRID = 16
TILE = 256
COLS = TILE // LAYERS
TOPS = 32
SIDE = 4
ROW_GROUPS = [[SIDE * x + y for y in range(SIDE)] for x in range(SIDE)]
COLUMN_GROUPS = [[SIDE * x + y for x in range(SIDE)] for y in range(SIDE)]
MIB = 1024 * 1024
HALF = TILE // 2

NN = (((1,), (0,)), ((), ()))
NT = (((1,), (1,)), ((), ()))

whole = pl.BlockSpec(memory_space=pltpu.VMEM)
in_hbm = pl.BlockSpec(memory_space=pl.ANY)


def split(value):
    high = value.astype(jnp.bfloat16)
    low = (value - high.astype(jnp.float32)).astype(jnp.bfloat16)
    return high, low


def product(left, right, dims):
    ((near,), (far,)), _ = dims
    wide = jnp.concatenate([left[0], left[0], left[1]], axis=near)
    tall = jnp.concatenate([right[0], right[1], right[0]], axis=far)
    return lax.dot_general(wide, tall, dims, preferred_element_type=jnp.float32)


far = pl.BlockSpec(memory_space=pltpu.HBM)


def params(mib):
    return pltpu.CompilerParams(vmem_limit_bytes=mib * MIB)


def cost(flops):
    return pl.CostEstimate(flops=flops, bytes_accessed=0, transcendentals=0)


def prepare_kernel(linv, lower, uinv, upper, rhs, fmat, bmat, share, rhs_t):
    core = lax.rem(lax.axis_index("layer"), 2)
    rows = pl.ds(pl.multiple_of(core * HALF, HALF), HALF)

    def maps(inverse, coupling, out):
        for i in range(2):
            out[i] = -product(split(inverse[i]), split(coupling[i]), NN)

    maps(linv, lower, fmat)
    share[0] = product(split(fmat[1, rows]), split(fmat[0]), NN)
    maps(uinv, upper, bmat)
    share[1] = product(split(bmat[0, rows]), split(bmat[1]), NN)
    for i in range(2):
        rhs_t[i] = rhs[i].T


def leaf_forward_kernel(targets, linv, rhs, low, fwd, *rest):
    outs, (acc, linv_in, rhs_in, low_in, fwd_out, in_sems, fwd_sems, sems) = rest[:10], rest[10:]
    leaves = linv.shape[0]
    layer = lax.axis_index("layer")
    core, z = lax.rem(layer, 2), lax.div(layer, 2)
    reads = [
        [
            pltpu.make_async_copy(source.at[k], held.at[k], in_sems.at[i, k])
            for i, (source, held) in enumerate(((linv, linv_in), (rhs, rhs_in), (low, low_in)))
        ]
        for k in range(leaves)
    ]
    for group in reads:
        for copy in group:
            copy.start()

    def clear(i, carry):
        acc[i] = jnp.zeros(acc.shape[1:], jnp.float32)
        return carry

    lax.fori_loop(0, acc.shape[0], clear, 0, unroll=8)
    writes = []
    for start in range(0, leaves, 2):
        pair = range(start, start + 2)
        for k in pair:
            for copy in reads[k]:
                copy.wait()
        turned = []
        for k in pair:
            value = product(split(linv_in[k]), split(rhs_in[k]), NN)
            fwd_out[k] = value
            turned.append(split(value.T))
        for k in pair:
            for c in range(2):
                t = targets[k, c]
                owner, odd = lax.div(t, 2), lax.rem(t, 2)
                coupled = product(turned[k - start], split(low_in[k, c]), NT)
                for goal in range(LAYERS):
                    side = lax.rem(goal % 2 + core, 2)
                    away = lax.rem(goal // 2 - z + 4, 4)
                    even_place = (side * 4 + away) * GRID + owner
                    odd_place = 8 * GRID + (side * GRID + owner) * 4 + away
                    acc[jnp.where(odd == 0, even_place, odd_place)] += coupled[
                        goal * COLS : (goal + 1) * COLS
                    ]
        for k in pair:
            writes.append(pltpu.make_async_copy(fwd_out.at[k], fwd.at[k], fwd_sems.at[k]))
            writes[-1].start()
    place = 0
    for i, out in enumerate(outs):
        size = out.shape[0]
        writes.append(pltpu.make_async_copy(acc.at[pl.ds(place, size)], out, sems.at[i]))
        writes[-1].start()
        place += size
    for copy in writes:
        copy.wait()


def leaf_forward(targets, linv, rhs, low):
    leaves = linv.shape[0]
    even = jax.ShapeDtypeStruct((GRID, COLS, TILE), jnp.float32)
    odd = jax.ShapeDtypeStruct((GRID * 4, COLS, TILE), jnp.float32)
    return pl.pallas_call(
        leaf_forward_kernel,
        out_shape=[jax.ShapeDtypeStruct(linv.shape, jnp.float32)] + [even] * 8 + [odd] * 2,
        in_specs=[pl.BlockSpec(memory_space=pltpu.SMEM)] + [far] * 3,
        out_specs=[far] * 11,
        scratch_shapes=[
            pltpu.VMEM((16 * GRID, COLS, TILE), jnp.float32),
            pltpu.VMEM(linv.shape, jnp.float32),
            pltpu.VMEM(rhs.shape, jnp.float32),
            pltpu.VMEM(low.shape, jnp.float32),
            pltpu.VMEM(linv.shape, jnp.float32),
            pltpu.SemaphoreType.DMA((3, leaves)),
            pltpu.SemaphoreType.DMA((leaves,)),
            pltpu.SemaphoreType.DMA((10,)),
        ],
        compiler_params=params(58),
        name="leaf_forward",
    )(targets, linv, rhs, low)


def gathered_kernel(first, second, third, fourth, out):
    out[...] = (first[...] + second[...]) + (third[...] + fourth[...])


def fold_kernel(parts, *outs):
    for i, out in enumerate(outs):
        total = parts[0, i]
        for g in range(1, GRID):
            total = total + parts[g, i]
        out[...] = total


def enter_kernel(even, odd, odd_1, odd_2, odd_3, rhs_t, linv, fmat, vec, spread):
    rows = pl.ds(pl.multiple_of(lax.axis_index("layer") * COLS, COLS), COLS)
    total = even[0]
    for g in range(1, GRID):
        total = total + even[g]
    first = product(split(rhs_t[0, rows] - total), split(linv[0]), NT)
    total = (odd[...] + odd_1[...]) + (odd_2[...] + odd_3[...])
    second = product(split(rhs_t[1, rows] - total), split(linv[1]), NT)
    vec[0] = first
    vec[1] = second
    last = second + product(split(first), split(fmat[1]), NT)
    for i in range(SIDE):
        spread[i] = last


def halves():
    core = lax.rem(lax.axis_index("layer"), 2)
    return [pl.ds(pl.multiple_of(side * HALF, HALF), HALF) for side in (core, 1 - core)]


def group_kernel(*refs):
    pieces, (forward, backward, share) = refs[: 2 * SIDE], refs[2 * SIDE :]
    y = lax.rem(lax.axis_index("grid"), SIDE)
    mine, theirs = halves()
    for which, out in enumerate((forward, backward)):
        for step in range(SIDE):
            place = lax.rem(y - step + SIDE, SIDE)
            out[place, mine] = pieces[step][which]
            out[place, theirs] = pieces[SIDE + step][which]
    for which, out, order in ((0, forward, (3, 2, 1, 0)), (1, backward, (0, 1, 2, 3))):
        made = out[order[0], mine]
        for i in order[1:]:
            made = product(split(made), split(out[i]), NN)
        share[which] = made


def total_kernel(order, values, steps, spread):
    carried = values[order[0]]
    for i in order[1:]:
        carried = values[i] + product(split(carried), split(steps[i]), NT)
    for i in range(SIDE):
        spread[i] = carried


def arriving(which, across, values, steps, own, other, states, held):
    mine, theirs = halves()
    for i in (1, 2):
        held[i, mine] = own[i, which]
        held[i, theirs] = other[i, which]
    x = lax.div(lax.axis_index("grid"), SIDE)
    y = lax.rem(lax.axis_index("grid"), SIDE)
    order, step = (list(range(SIDE)), 1) if which == 0 else (list(range(SIDE))[::-1], -1)
    carried = jnp.zeros(states.shape[1:], jnp.float32)
    states[order[0]] = carried
    for i in order[:-1]:
        carried = across[i] if i == order[0] else across[i] + product(split(carried), split(held[i]), NT)
        states[i + step] = carried
    carried = states[x]
    states[SIDE + order[0]] = carried
    for i in order[:-1]:
        carried = values[i] + product(split(carried), split(steps[i]), NT)
        states[SIDE + i + step] = carried
    return states[SIDE + y]


def turn_kernel(across, values, steps, own, other, vec, fmat, uinv, bmat, out, spread, states, held):
    incoming = arriving(0, across, values, steps, own, other, states, held)
    first = vec[0] + product(split(incoming), split(fmat[0]), NT)
    second = vec[1] + product(split(first), split(fmat[1]), NT)
    upper_second = product(split(second), split(uinv[1]), NT)
    upper_first = product(split(first), split(uinv[0]), NT)
    out[0] = upper_first
    out[1] = upper_second
    last = upper_first + product(split(upper_second), split(bmat[0]), NT)
    for i in range(SIDE):
        spread[i] = last


def leave_kernel(across, values, steps, own, other, vec, bmat, even, spread, states, held):
    incoming = arriving(1, across, values, steps, own, other, states, held)
    second = vec[1] + product(split(incoming), split(bmat[1]), NT)
    even[...] = vec[0] + product(split(second), split(bmat[0]), NT)
    for g in range(GRID):
        spread[g] = second


def copies_kernel(first, second, third, fourth, spread):
    z = lax.div(lax.axis_index("layer"), 2)
    for d, value in enumerate((first, second, third, fourth)):
        for g in range(GRID):
            spread[g, lax.rem(z - d + 4, 4)] = value[...]


def leaf_ready_kernel(uinv, up, fwd, base, factor):
    for leaf in range(uinv.shape[0]):
        inverse = split(uinv[leaf])
        base[leaf] = product(inverse, split(fwd[leaf]), NN)
        for c in range(2):
            factor[leaf, c] = product(inverse, split(up[leaf, c]), NN)


def leaf_ready(uinv, up, fwd, step=2):
    tile = pl.BlockSpec((step, TILE, TILE), lambda k: (k, 0, 0))
    pair = pl.BlockSpec((step, 2, TILE, TILE), lambda k: (k, 0, 0, 0))
    return pl.pallas_call(
        leaf_ready_kernel,
        out_shape=[jax.ShapeDtypeStruct(x.shape, jnp.float32) for x in (uinv, up)],
        grid=(uinv.shape[0] // step,),
        in_specs=[tile, pair, tile],
        out_specs=[tile, pair],
        compiler_params=params(20),
        name="leaf_ready",
    )(uinv, up, fwd)


def leaf_back_kernel(
    targets, base, factor, even, even_other, odd, out, own,
    solved, base_in, factor_in, out_held, own_held, sems, in_sems, out_sems,
):
    leaves = base.shape[0]
    core = lax.rem(lax.axis_index("layer"), 2)

    def read(slot, t):
        owner = lax.div(t, 2)

        @pl.when(lax.rem(t, 2) == 1)
        def _():
            pltpu.make_async_copy(odd.at[:, :, owner], solved.at[slot], sems.at[slot]).start()

        @pl.when(lax.rem(t, 2) == 0)
        def _():
            for source, side in ((even, core), (even_other, 1 - core)):
                pltpu.make_async_copy(
                    source.at[owner], solved.at[slot, :, side], sems.at[slot]
                ).start()

    def ready(slot):
        pltpu.make_async_copy(odd.at[:, :, 0], solved.at[slot], sems.at[slot]).wait()

    reads = []
    for k in range(leaves):
        for c in range(2):
            read(2 * k + c, targets[k, c])
        reads.append(
            [
                pltpu.make_async_copy(base.at[k], base_in.at[k], in_sems.at[0, k]),
                pltpu.make_async_copy(factor.at[k], factor_in.at[k], in_sems.at[1, k]),
            ]
        )
        for copy in reads[k]:
            copy.start()
    for i in range(2):
        read(2 * leaves + i, 2 * lax.axis_index("grid") + i)

    writes = []
    for start in range(0, leaves, 2):
        pair = range(start, start + 2)
        for k in pair:
            for copy in reads[k]:
                copy.wait()
            for c in range(2):
                ready(2 * k + c)
        for k in pair:
            value = base_in[k]
            for c in range(2):
                picked = solved[2 * k + c].reshape(TILE, TILE)
                value = value - product(split(factor_in[k, c]), split(picked), NT)
            out_held[k] = value
        for k in pair:
            writes.append(pltpu.make_async_copy(out_held.at[k], out.at[k], out_sems.at[k]))
            writes[-1].start()
    for i in range(2):
        ready(2 * leaves + i)
        own_held[i] = solved[2 * leaves + i].reshape(TILE, TILE).T
    writes.append(pltpu.make_async_copy(own_held, own, out_sems.at[leaves]))
    writes[-1].start()
    for copy in writes:
        copy.wait()


def leaf_back(targets, base, factor, even, odd):
    leaves = base.shape[0]
    two = (2, TILE, TILE)
    return pl.pallas_call(
        leaf_back_kernel,
        out_shape=[
            jax.ShapeDtypeStruct(base.shape, jnp.float32),
            jax.ShapeDtypeStruct(two, jnp.float32),
        ],
        in_specs=[pl.BlockSpec(memory_space=pltpu.SMEM)] + [far] * 2 + [in_hbm] * 2 + [far],
        out_specs=[far] * 2,
        scratch_shapes=[
            pltpu.VMEM((2 * leaves + 2, 4, 2, COLS, TILE), jnp.float32),
            pltpu.VMEM(base.shape, jnp.float32),
            pltpu.VMEM(factor.shape, jnp.float32),
            pltpu.VMEM(base.shape, jnp.float32),
            pltpu.VMEM(two, jnp.float32),
            pltpu.SemaphoreType.DMA((2 * leaves + 2,)),
            pltpu.SemaphoreType.DMA((2, leaves)),
            pltpu.SemaphoreType.DMA((leaves + 1,)),
        ],
        compiler_params=params(58),
        name="leaf_back",
    )(targets, base, factor, *even, odd)


def call(kernel, outs, name, *args, scratch=(), mib=10, hint=1_000_000):
    return pl.pallas_call(
        kernel,
        out_shape=[jax.ShapeDtypeStruct(shape, jnp.float32) for shape in outs],
        in_specs=[whole] * len(args),
        out_specs=[whole] * len(outs),
        scratch_shapes=list(scratch),
        compiler_params=params(mib),
        cost_estimate=cost(hint),
        name=name,
    )(*args)


def after(values):
    return lax.optimization_barrier(values)


def other_core(value):
    return lax.ppermute(value, "layer", [(i, i + 1 - 2 * (i % 2)) for i in range(LAYERS)])


def along_z(value, steps):
    return lax.ppermute(value, "layer", [(i, (i + 2 * steps) % LAYERS) for i in range(LAYERS)])


def along_y(value, steps):
    pairs = [
        (SIDE * x + y, SIDE * x + (y + steps) % SIDE) for x in range(SIDE) for y in range(SIDE)
    ]
    return lax.ppermute(value, "grid", pairs)


def within(value, groups):
    return lax.all_to_all(
        value, "grid", split_axis=0, concat_axis=0, axis_index_groups=groups, tiled=True
    )


def exchange(value):
    return lax.all_to_all(value, "grid", split_axis=0, concat_axis=0, tiled=True)


def local(
    leaf_rhs,
    leaf_linv,
    leaf_uinv,
    low_couple,
    up_couple,
    targets,
    top_rhs,
    top_linv,
    top_uinv,
    top_lower,
    top_upper,
):
    two = (2, TILE, TILE)
    slim = (2, COLS, TILE)
    slip = (COLS, TILE)
    spread = (GRID, COLS, TILE)

    tops = (top_linv, top_lower, top_uinv, top_upper, top_rhs)
    fmat, bmat, share, rhs_t = call(
        prepare_kernel, [two, two, (2, HALF, TILE), two], "prepare", *tops, mib=56
    )
    share, leaf_rhs = after((share, leaf_rhs))
    rows = [share] + [along_y(share, step) for step in range(1, SIDE)]
    fwd, *parts = leaf_forward(targets, leaf_linv, leaf_rhs, low_couple)
    even_keep, even_send, odd_keep, odd_send = parts[:4], parts[4:8], parts[8], parts[9]
    odd = exchange(odd_keep + other_core(odd_send)).reshape(GRID, 4, COLS, TILE)
    even = [even_keep[d] + other_core(even_send[d]) for d in (1, 2, 3, 0)]
    rows = rows + [other_core(piece) for piece in rows]
    even = [even[3]] + [along_z(even[d - 1], d) for d in range(1, 4)]
    [even] = call(gathered_kernel, [spread], "gathered", *even)
    even, odd = after((even, odd))
    odd = call(fold_kernel, [slip] * 4, "fold", odd)
    odd, rows = after((odd, rows))
    four = (SIDE, TILE, TILE)
    forward, backward, share = call(
        group_kernel, [four, four, (2, HALF, TILE)], "group", *rows
    )
    columns = lax.all_gather(share, "grid", axis=0, axis_index_groups=COLUMN_GROUPS)
    odd = [odd[0]] + [along_z(odd[d], d) for d in range(1, 4)]
    even = exchange(even)

    small = (SIDE, COLS, TILE)
    vec, sent = call(enter_kernel, [slim, small], "enter", even, *odd, rhs_t, tops[0], fmat)
    values = within(sent, ROW_GROUPS)
    states = [
        pltpu.VMEM((2 * SIDE, COLS, TILE), jnp.float32),
        pltpu.VMEM(four, jnp.float32),
    ]
    up_order, down_order = list(range(SIDE)), list(range(SIDE))[::-1]
    [sent] = call(functools.partial(total_kernel, up_order), [small], "total", values, forward)
    sent, columns = after((sent, columns))
    columns = (columns, other_core(columns))
    across = within(sent, COLUMN_GROUPS)
    vec, sent = call(
        turn_kernel,
        [slim, small],
        "turn",
        *(across, values, forward, *columns, vec, fmat, tops[2], bmat),
        scratch=states,
    )
    values = within(sent, ROW_GROUPS)
    [sent] = call(functools.partial(total_kernel, down_order), [small], "total", values, backward)
    across = within(sent, COLUMN_GROUPS)
    even, sent = call(
        leave_kernel,
        [slip, spread],
        "leave",
        *(across, values, backward, *columns, vec, bmat),
        scratch=states,
    )
    even = [even] + [along_z(even, d) for d in range(1, 4)]
    [even] = call(copies_kernel, [(GRID, 4, COLS, TILE)], "copies", *even)
    odd = exchange(sent)
    even, odd, leaf_uinv = after((even, odd, leaf_uinv))
    base, factor = leaf_ready(leaf_uinv, up_couple, fwd)
    odd = lax.all_gather(odd, "layer", axis=0, tiled=False).reshape(4, 2, *spread)
    even = exchange(even.reshape(GRID * 4, COLS, TILE)).reshape(GRID, 4, COLS, TILE)
    even, base, factor = after((even, base, factor))
    even = [even, other_core(even)]
    return tuple(leaf_back(targets, base, factor, even, odd))


def solution(mesh):
    leaf = P(("layer", "grid"), None, None)
    leaf_pair = P(("layer", "grid"), None, None, None)
    top = P("grid", None, None)
    return jax.shard_map(
        local,
        mesh=mesh,
        in_specs=(leaf, leaf, leaf, leaf_pair, leaf_pair, P(("layer", "grid"), None))
        + (top,) * 5,
        out_specs=(leaf, top),
        check_vma=False,
    )
```

```python
import jax
import jax.numpy as jnp
from jax import lax
from jax.experimental import pallas as pl
from jax.experimental.pallas import tpu as pltpu
from jax.sharding import PartitionSpec as P

LAYERS = 8
GRID = 16
TILE = 256
COLS = TILE // LAYERS
TOPS = 32
MIB = 1024 * 1024
HALF = TILE // 2

NN = (((1,), (0,)), ((), ()))
NT = (((1,), (1,)), ((), ()))

whole = pl.BlockSpec(memory_space=pltpu.VMEM)
in_hbm = pl.BlockSpec(memory_space=pl.ANY)


def split(value):
    high = value.astype(jnp.bfloat16)
    low = (value - high.astype(jnp.float32)).astype(jnp.bfloat16)
    return high, low


def product(left, right, dims):
    ((near,), (far,)), _ = dims
    wide = jnp.concatenate([left[0], left[0], left[1]], axis=near)
    tall = jnp.concatenate([right[0], right[1], right[0]], axis=far)
    return lax.dot_general(wide, tall, dims, preferred_element_type=jnp.float32)


far = pl.BlockSpec(memory_space=pltpu.HBM)


def params(mib):
    return pltpu.CompilerParams(vmem_limit_bytes=mib * MIB)


def cost(flops):
    return pl.CostEstimate(flops=flops, bytes_accessed=0, transcendentals=0)


def prepare_kernel(linv, lower, uinv, upper, rhs, fmat, bmat, share, rhs_t):
    core = lax.rem(lax.axis_index("layer"), 2)
    rows = pl.ds(pl.multiple_of(core * HALF, HALF), HALF)

    def maps(inverse, coupling, out):
        for i in range(2):
            out[i] = -product(split(inverse[i]), split(coupling[i]), NN)

    maps(linv, lower, fmat)
    share[0] = product(split(fmat[1, rows]), split(fmat[0]), NN)
    maps(uinv, upper, bmat)
    share[1] = product(split(bmat[0, rows]), split(bmat[1]), NN)
    for i in range(2):
        rhs_t[i] = rhs[i].T


def leaf_forward_kernel(targets, linv, rhs, low, fwd, *rest):
    outs, (acc, linv_in, rhs_in, low_in, fwd_out, in_sems, fwd_sems, sems) = rest[:10], rest[10:]
    leaves = linv.shape[0]
    layer = lax.axis_index("layer")
    core, z = lax.rem(layer, 2), lax.div(layer, 2)
    reads = [
        [
            pltpu.make_async_copy(source.at[k], held.at[k], in_sems.at[i, k])
            for i, (source, held) in enumerate(((linv, linv_in), (rhs, rhs_in), (low, low_in)))
        ]
        for k in range(leaves)
    ]
    for group in reads:
        for copy in group:
            copy.start()

    def clear(i, carry):
        acc[i] = jnp.zeros(acc.shape[1:], jnp.float32)
        return carry

    lax.fori_loop(0, acc.shape[0], clear, 0, unroll=8)
    writes = []
    for start in range(0, leaves, 2):
        pair = range(start, start + 2)
        for k in pair:
            for copy in reads[k]:
                copy.wait()
        turned = []
        for k in pair:
            value = product(split(linv_in[k]), split(rhs_in[k]), NN)
            fwd_out[k] = value
            turned.append(split(value.T))
        for k in pair:
            for c in range(2):
                t = targets[k, c]
                owner, odd = lax.div(t, 2), lax.rem(t, 2)
                coupled = product(turned[k - start], split(low_in[k, c]), NT)
                for goal in range(LAYERS):
                    side = lax.rem(goal % 2 + core, 2)
                    away = lax.rem(goal // 2 - z + 4, 4)
                    even_place = (side * 4 + away) * GRID + owner
                    odd_place = 8 * GRID + (side * GRID + owner) * 4 + away
                    acc[jnp.where(odd == 0, even_place, odd_place)] += coupled[
                        goal * COLS : (goal + 1) * COLS
                    ]
        for k in pair:
            writes.append(pltpu.make_async_copy(fwd_out.at[k], fwd.at[k], fwd_sems.at[k]))
            writes[-1].start()
    place = 0
    for i, out in enumerate(outs):
        size = out.shape[0]
        writes.append(pltpu.make_async_copy(acc.at[pl.ds(place, size)], out, sems.at[i]))
        writes[-1].start()
        place += size
    for copy in writes:
        copy.wait()


def leaf_forward(targets, linv, rhs, low):
    leaves = linv.shape[0]
    even = jax.ShapeDtypeStruct((GRID, COLS, TILE), jnp.float32)
    odd = jax.ShapeDtypeStruct((GRID * 4, COLS, TILE), jnp.float32)
    return pl.pallas_call(
        leaf_forward_kernel,
        out_shape=[jax.ShapeDtypeStruct(linv.shape, jnp.float32)] + [even] * 8 + [odd] * 2,
        in_specs=[pl.BlockSpec(memory_space=pltpu.SMEM)] + [far] * 3,
        out_specs=[far] * 11,
        scratch_shapes=[
            pltpu.VMEM((16 * GRID, COLS, TILE), jnp.float32),
            pltpu.VMEM(linv.shape, jnp.float32),
            pltpu.VMEM(rhs.shape, jnp.float32),
            pltpu.VMEM(low.shape, jnp.float32),
            pltpu.VMEM(linv.shape, jnp.float32),
            pltpu.SemaphoreType.DMA((3, leaves)),
            pltpu.SemaphoreType.DMA((leaves,)),
            pltpu.SemaphoreType.DMA((10,)),
        ],
        compiler_params=params(58),
        name="leaf_forward",
    )(targets, linv, rhs, low)


def joined_kernel(first, second, out):
    out[...] = first[...] + second[...]


def joined(first, second, steps=4):
    block = pl.BlockSpec((first.shape[0] // steps, COLS, TILE), lambda i: (i, 0, 0))
    return pl.pallas_call(
        joined_kernel,
        out_shape=jax.ShapeDtypeStruct(first.shape, jnp.float32),
        grid=(steps,),
        in_specs=[block] * 2,
        out_specs=block,
        compiler_params=params(20),
        name="joined",
    )(first, second)


def gathered_kernel(first, second, third, fourth, out):
    out[...] = (first[...] + second[...]) + (third[...] + fourth[...])


def fold_kernel(parts, *outs):
    for i, out in enumerate(outs):
        total = parts[0, i]
        for g in range(1, GRID):
            total = total + parts[g, i]
        out[...] = total


def enter_kernel(even, odd, odd_1, odd_2, odd_3, rhs_t, linv, fmat, vec, spread):
    rows = pl.ds(pl.multiple_of(lax.axis_index("layer") * COLS, COLS), COLS)
    total = even[0]
    for g in range(1, GRID):
        total = total + even[g]
    first = product(split(rhs_t[0, rows] - total), split(linv[0]), NT)
    total = (odd[...] + odd_1[...]) + (odd_2[...] + odd_3[...])
    second = product(split(rhs_t[1, rows] - total), split(linv[1]), NT)
    vec[0] = first
    vec[1] = second
    last = second + product(split(first), split(fmat[1]), NT)
    for g in range(GRID):
        spread[g] = last


def chain_kernel(own, other, forward, backward):
    core = lax.rem(lax.axis_index("layer"), 2)
    for i, source in enumerate((own, other)):
        side = core if i == 0 else 1 - core
        rows = pl.ds(pl.multiple_of(side * HALF, HALF), HALF)
        for h in range(1, GRID - 1):
            for which, out in enumerate((forward, backward)):
                high, low = split(source[2 * h + which])
                out[0, h, rows] = high
                out[1, h, rows] = low


def chain_pairs(own, other):
    pairs = jax.ShapeDtypeStruct((2, GRID, TILE, TILE), jnp.bfloat16)
    return pl.pallas_call(
        chain_kernel,
        out_shape=[pairs, pairs],
        in_specs=[whole] * 2,
        out_specs=[whole] * 2,
        compiler_params=params(20),
        name="chain_pairs",
    )(own, other)


def turn_kernel(values, chain, vec, fmat, uinv, bmat, out, spread, states):
    states[0] = jnp.zeros(states.shape[1:], jnp.float32)
    states[1] = values[0]
    carried = values[0]
    for h in range(1, GRID - 1):
        carried = values[h] + product(split(carried), (chain[0, h], chain[1, h]), NT)
        states[h + 1] = carried
    incoming = states[lax.axis_index("grid")]
    first = vec[0] + product(split(incoming), split(fmat[0]), NT)
    second = vec[1] + product(split(first), split(fmat[1]), NT)
    upper_second = product(split(second), split(uinv[1]), NT)
    upper_first = product(split(first), split(uinv[0]), NT)
    out[0] = upper_first
    out[1] = upper_second
    last = upper_first + product(split(upper_second), split(bmat[0]), NT)
    for g in range(GRID):
        spread[g] = last


def leave_kernel(values, chain, vec, bmat, even, spread, states):
    states[GRID - 1] = jnp.zeros(states.shape[1:], jnp.float32)
    states[GRID - 2] = values[GRID - 1]
    carried = values[GRID - 1]
    for h in range(GRID - 2, 0, -1):
        carried = values[h] + product(split(carried), (chain[0, h], chain[1, h]), NT)
        states[h - 1] = carried
    incoming = states[lax.axis_index("grid")]
    second = vec[1] + product(split(incoming), split(bmat[1]), NT)
    even[...] = vec[0] + product(split(second), split(bmat[0]), NT)
    for g in range(GRID):
        spread[g] = second


def copies_kernel(first, second, third, fourth, spread):
    z = lax.div(lax.axis_index("layer"), 2)
    for d, value in enumerate((first, second, third, fourth)):
        for g in range(GRID):
            spread[g, lax.rem(z - d + 4, 4)] = value[...]


def leaf_ready_kernel(uinv, up, fwd, base, factor):
    for leaf in range(uinv.shape[0]):
        inverse = split(uinv[leaf])
        base[leaf] = product(inverse, split(fwd[leaf]), NN)
        for c in range(2):
            factor[leaf, c] = product(inverse, split(up[leaf, c]), NN)


def leaf_ready(uinv, up, fwd, step=2):
    tile = pl.BlockSpec((step, TILE, TILE), lambda k: (k, 0, 0))
    pair = pl.BlockSpec((step, 2, TILE, TILE), lambda k: (k, 0, 0, 0))
    return pl.pallas_call(
        leaf_ready_kernel,
        out_shape=[jax.ShapeDtypeStruct(x.shape, jnp.float32) for x in (uinv, up)],
        grid=(uinv.shape[0] // step,),
        in_specs=[tile, pair, tile],
        out_specs=[tile, pair],
        compiler_params=params(20),
        name="leaf_ready",
    )(uinv, up, fwd)


def leaf_back_kernel(
    targets, base, factor, even, even_other, odd, out, own,
    solved, base_in, factor_in, out_held, own_held, sems, in_sems, out_sems,
):
    leaves = base.shape[0]
    core = lax.rem(lax.axis_index("layer"), 2)

    def read(slot, t):
        owner = lax.div(t, 2)

        @pl.when(lax.rem(t, 2) == 1)
        def _():
            pltpu.make_async_copy(odd.at[:, :, owner], solved.at[slot], sems.at[slot]).start()

        @pl.when(lax.rem(t, 2) == 0)
        def _():
            for source, side in ((even, core), (even_other, 1 - core)):
                pltpu.make_async_copy(
                    source.at[owner], solved.at[slot, :, side], sems.at[slot]
                ).start()

    def ready(slot):
        pltpu.make_async_copy(odd.at[:, :, 0], solved.at[slot], sems.at[slot]).wait()

    reads = []
    for k in range(leaves):
        for c in range(2):
            read(2 * k + c, targets[k, c])
        reads.append(
            [
                pltpu.make_async_copy(base.at[k], base_in.at[k], in_sems.at[0, k]),
                pltpu.make_async_copy(factor.at[k], factor_in.at[k], in_sems.at[1, k]),
            ]
        )
        for copy in reads[k]:
            copy.start()
    for i in range(2):
        read(2 * leaves + i, 2 * lax.axis_index("grid") + i)

    writes = []
    for start in range(0, leaves, 2):
        pair = range(start, start + 2)
        for k in pair:
            for copy in reads[k]:
                copy.wait()
            for c in range(2):
                ready(2 * k + c)
        for k in pair:
            value = base_in[k]
            for c in range(2):
                picked = solved[2 * k + c].reshape(TILE, TILE)
                value = value - product(split(factor_in[k, c]), split(picked), NT)
            out_held[k] = value
        for k in pair:
            writes.append(pltpu.make_async_copy(out_held.at[k], out.at[k], out_sems.at[k]))
            writes[-1].start()
    for i in range(2):
        ready(2 * leaves + i)
        own_held[i] = solved[2 * leaves + i].reshape(TILE, TILE).T
    writes.append(pltpu.make_async_copy(own_held, own, out_sems.at[leaves]))
    writes[-1].start()
    for copy in writes:
        copy.wait()


def leaf_back(targets, base, factor, even, odd):
    leaves = base.shape[0]
    two = (2, TILE, TILE)
    return pl.pallas_call(
        leaf_back_kernel,
        out_shape=[
            jax.ShapeDtypeStruct(base.shape, jnp.float32),
            jax.ShapeDtypeStruct(two, jnp.float32),
        ],
        in_specs=[pl.BlockSpec(memory_space=pltpu.SMEM)] + [far] * 2 + [in_hbm] * 2 + [far],
        out_specs=[far] * 2,
        scratch_shapes=[
            pltpu.VMEM((2 * leaves + 2, 4, 2, COLS, TILE), jnp.float32),
            pltpu.VMEM(base.shape, jnp.float32),
            pltpu.VMEM(factor.shape, jnp.float32),
            pltpu.VMEM(base.shape, jnp.float32),
            pltpu.VMEM(two, jnp.float32),
            pltpu.SemaphoreType.DMA((2 * leaves + 2,)),
            pltpu.SemaphoreType.DMA((2, leaves)),
            pltpu.SemaphoreType.DMA((leaves + 1,)),
        ],
        compiler_params=params(58),
        name="leaf_back",
    )(targets, base, factor, *even, odd)


def call(kernel, outs, name, *args, scratch=(), mib=10, hint=1_000_000):
    return pl.pallas_call(
        kernel,
        out_shape=[jax.ShapeDtypeStruct(shape, jnp.float32) for shape in outs],
        in_specs=[whole] * len(args),
        out_specs=[whole] * len(outs),
        scratch_shapes=list(scratch),
        compiler_params=params(mib),
        cost_estimate=cost(hint),
        name=name,
    )(*args)


def after(values):
    return lax.optimization_barrier(values)


def other_core(value):
    return lax.ppermute(value, "layer", [(i, i + 1 - 2 * (i % 2)) for i in range(LAYERS)])


def along_z(value, steps):
    return lax.ppermute(value, "layer", [(i, (i + 2 * steps) % LAYERS) for i in range(LAYERS)])


def exchange(value):
    return lax.all_to_all(value, "grid", split_axis=0, concat_axis=0, tiled=True)


def local(
    leaf_rhs,
    leaf_linv,
    leaf_uinv,
    low_couple,
    up_couple,
    targets,
    top_rhs,
    top_linv,
    top_uinv,
    top_lower,
    top_upper,
):
    two = (2, TILE, TILE)
    slim = (2, COLS, TILE)
    piece = (COLS, TILE)
    spread = (GRID, COLS, TILE)

    tops = (top_linv, top_lower, top_uinv, top_upper, top_rhs)
    fmat, bmat, share, rhs_t = call(
        prepare_kernel, [two, two, (2, HALF, TILE), two], "prepare", *tops, mib=56
    )
    share, leaf_rhs = after((share, leaf_rhs))
    chain = lax.all_gather(share, "grid", axis=0, tiled=True)
    fwd, *parts = leaf_forward(targets, leaf_linv, leaf_rhs, low_couple)
    even_keep, even_send, odd_keep, odd_send = parts[:4], parts[4:8], parts[8], parts[9]
    even = [even_keep[d] + other_core(even_send[d]) for d in (1, 2, 3, 0)]
    odd = joined(odd_keep, other_core(odd_send))
    odd, leaf_uinv = after((odd, leaf_uinv))
    odd = exchange(odd).reshape(GRID, 4, COLS, TILE)
    base, factor = leaf_ready(leaf_uinv, up_couple, fwd)
    even = [even[3]] + [along_z(even[d - 1], d) for d in range(1, 4)]
    [even] = call(gathered_kernel, [spread], "gathered", *even)
    even, base, factor = after((even, base, factor))
    even, odd = after((even, odd))
    odd = call(fold_kernel, [piece] * 4, "fold", odd)
    odd = [odd[0]] + [along_z(odd[d], d) for d in range(1, 4)]
    even = exchange(even)

    vec, sent = call(
        enter_kernel, [slim, spread], "enter", even, *odd, rhs_t, tops[0], fmat
    )
    vec, sent, chain = after((vec, sent, chain))
    forward, backward = chain_pairs(chain, other_core(chain))
    values = exchange(sent)
    values, forward, backward = after((values, forward, backward))
    states = [pltpu.VMEM(spread, jnp.float32)]
    vec, sent = call(
        turn_kernel,
        [slim, spread],
        "turn",
        *(values, forward, vec, fmat, tops[2], bmat),
        scratch=states,
        mib=10,
    )
    values = exchange(sent)
    even, sent = call(
        leave_kernel,
        [piece, spread],
        "leave",
        *(values, backward, vec, bmat),
        scratch=states,
        mib=10,
    )
    even = [even] + [along_z(even, d) for d in range(1, 4)]
    [even] = call(copies_kernel, [(GRID, 4, COLS, TILE)], "copies", *even)
    odd = exchange(sent)
    even, odd = after((even, odd))
    odd = lax.all_gather(odd, "layer", axis=0, tiled=False).reshape(4, 2, *spread)
    even = exchange(even.reshape(GRID * 4, COLS, TILE)).reshape(GRID, 4, COLS, TILE)
    even = [even, other_core(even)]
    return tuple(leaf_back(targets, base, factor, even, odd))


def solution(mesh):
    leaf = P(("layer", "grid"), None, None)
    leaf_pair = P(("layer", "grid"), None, None, None)
    top = P("grid", None, None)
    return jax.shard_map(
        local,
        mesh=mesh,
        in_specs=(leaf, leaf, leaf, leaf_pair, leaf_pair, P(("layer", "grid"), None))
        + (top,) * 5,
        out_specs=(leaf, top),
        check_vma=False,
    )
```
